512 devices in a mesh: ctx: 128 (over x, z, core), head: 4 (over y).
Axes of the slice: x: 4, y: 4, z: 16, core: 2. Of those that a mesh axis runs over, the one named last changes fastest.
Arguments:
- queries: bfloat16 [16384, 4096], P('ctx', 'head'), may hold values from -6 to 6
- keys: bfloat16 [16384, 4096], P('ctx', 'head'), may hold values from -6 to 6
- values: bfloat16 [16384, 4096], P('ctx', 'head'), may hold values from -60 to 60
- gain: float32 [4096], P('head'), may hold values from 0.1 to 1.9
- cotangent: bfloat16 [16384, 4096], P('ctx', 'head'), may hold values from -6 to 6
Outputs:
- normed: bfloat16 [16384, 4096], P('ctx', 'head')
- grad_queries: bfloat16 [16384, 4096], P('ctx', 'head')
- grad_keys: bfloat16 [16384, 4096], P('ctx', 'head')
- grad_values: bfloat16 [16384, 4096], P('ctx', 'head')
The draws below stay inside these ranges and needn't reach their ends.
All inputs are finite; a program needn't handle non-finite values.
Results may differ from the reference program's by a relative error of at most 0.0065.
Values may be sent and summed in bfloat16 or wider, within the bound.
No kernel may reach another device: no remote copies, remote signals or barrier semaphores. Data moves between devices by JAX's collectives and lax.ppermute only.
A program may use at most 192 MiB of HBM per device.

```python
import jax
import jax.numpy as jnp
from jax import lax

TOK_DEV = 128
HEADS = 32
DH = 128
SEQ = 16384


def draw_values(key, part):
    key = jax.random.fold_in(key, 5)
    base_key, jitter_key = jax.random.split(key)
    columns = HEADS * DH
    head_of = (jnp.arange(columns) // DH).astype(jnp.float32)
    ramp = head_of / max(HEADS - 1, 1)
    jitter = jax.random.uniform(jitter_key, (columns,), minval=0.0, maxval=1.0)
    base = jnp.clip(jax.random.normal(base_key, (SEQ, columns)), -5.0, 5.0)
    scaling = jnp.exp(ramp * jnp.log(3.0) + jitter * jnp.log(3.4))
    return (base * scaling[None, :]).astype(jnp.float32).astype(jnp.bfloat16)


def steps_of(key, extent, cuts, smallest, top_value):
    level = 1.0
    for axis_at, parts in cuts:
        draws = jax.random.uniform(jax.random.fold_in(jax.random.fold_in(key, 6), axis_at), (parts,), jnp.float32, smallest / len(cuts), top_value / len(cuts))
        level = level * jnp.repeat(jnp.exp(draws), extent[axis_at] // parts).reshape((-1,) + (1,) * (len(extent) - 1 - axis_at))
    return level


def bell_draw(stream_key, dims, deviation, bound, cuts=(), kind=jnp.bfloat16):
    drawn = jax.random.normal(stream_key, dims, jnp.float32) * deviation
    if len(cuts) > 0:
        drawn = steps_of(stream_key, dims, cuts, -0.22, 0.18) * drawn
    return jnp.clip(drawn, min=-bound, max=bound).astype(kind)


def setup_inputs(seed: int = 0) -> dict:
    streams_of = jax.random.split(jax.random.key(seed), 6)
    return {
        "queries": bell_draw(streams_of[0], (SEQ, HEADS * DH), 1.0, 6.0, ((0, 128), (1, 4))),
        "keys": bell_draw(streams_of[1], (SEQ, HEADS * DH), 1.0, 6.0, ((0, 128), (1, 4))),
        "values": draw_values(jax.random.fold_in(streams_of[5], 71), 0),
        "gain": jnp.clip(1.0 + 0.18 * jax.random.normal(streams_of[3], (HEADS * DH,), jnp.float32), 0.1, 1.9),
        "cotangent": bell_draw(streams_of[4], (SEQ, HEADS * DH), 1.0, 6.0, ((0, 128), (1, 4))),
    }


EPSILON = 1e-06

def block_parts(matrix):
    return matrix.reshape(SEQ // TOK_DEV, TOK_DEV, HEADS, DH)

def reference(queries, keys, values, gain, cotangent):
    blocks = SEQ // TOK_DEV
    columns = HEADS * DH
    query_blocks = block_parts(queries)
    key_blocks = block_parts(keys)
    value_blocks = block_parts(values)
    grad_blocks = block_parts(cotangent)
    causal = jnp.tril(jnp.ones((TOK_DEV, TOK_DEV), dtype=bool))
    scaling = gain.astype(jnp.float32)

    def state_of(pieces):
        key_heads, value_heads = pieces
        return jnp.einsum('tha,thc->hac', key_heads.astype(jnp.float32), value_heads.astype(jnp.float32))
    states = lax.map(state_of, (key_blocks, value_blocks))
    zeros = jnp.zeros((1,) + states.shape[1:], jnp.float32)
    before = jnp.concatenate([zeros, jnp.cumsum(states, axis=0)[:-1]], axis=0).astype(jnp.bfloat16)

    def forward_block(pieces):
        query_heads, key_heads, value_heads, grad_heads, before_block = pieces
        query_wide = query_heads.astype(jnp.float32)
        raw = jnp.einsum('tha,sha->hts', query_wide, key_heads.astype(jnp.float32))
        scores = jnp.where(causal[None], raw, 0.0).astype(jnp.bfloat16)
        inside = jnp.einsum('hts,shc->thc', scores.astype(jnp.float32), value_heads.astype(jnp.float32))
        carried = jnp.einsum('tha,hac->thc', query_wide, before_block.astype(jnp.float32))
        attended = (inside + carried).reshape(TOK_DEV, columns)
        inverse = lax.rsqrt(lax.optimization_barrier(jnp.sum(attended * attended, axis=1)) / columns + EPSILON)
        normed = (attended * inverse[:, None] * scaling).astype(jnp.bfloat16)
        weighted = grad_heads.reshape(TOK_DEV, columns).astype(jnp.float32) * scaling
        crossed = lax.optimization_barrier(jnp.sum(weighted * attended, axis=1)) / columns
        grad_attended = (inverse[:, None] * weighted - (inverse * inverse * inverse * crossed)[:, None] * attended).astype(jnp.bfloat16)
        grad_heads_att = grad_attended.reshape(TOK_DEV, HEADS, DH).astype(jnp.float32)
        products = jnp.einsum('tha,thc->hac', query_wide, grad_heads_att)
        return (normed, grad_attended, products)
    normed, grad_attended, products = lax.map(forward_block, (query_blocks, key_blocks, value_blocks, grad_blocks, before))
    reversed_sums = jnp.cumsum(products[::-1], axis=0)[::-1]
    beyond = jnp.concatenate([reversed_sums[1:], zeros], axis=0).astype(jnp.bfloat16)
    grad_att_blocks = grad_attended.reshape(blocks, TOK_DEV, HEADS, DH)

    def backward_block(pieces):
        query_heads, key_heads, value_heads, grad_heads, before_block, beyond_block = pieces
        query_wide = query_heads.astype(jnp.float32)
        key_wide = key_heads.astype(jnp.float32)
        value_wide = value_heads.astype(jnp.float32)
        grad_wide = grad_heads.astype(jnp.float32)
        raw = jnp.einsum('tha,sha->hts', query_wide, key_wide)
        scores = jnp.where(causal[None], raw, 0.0).astype(jnp.bfloat16).astype(jnp.float32)
        raw_grad = jnp.einsum('thc,shc->hts', grad_wide, value_wide)
        grad_scores = jnp.where(causal[None], raw_grad, 0.0).astype(jnp.bfloat16).astype(jnp.float32)
        before_wide = before_block.astype(jnp.float32)
        beyond_wide = beyond_block.astype(jnp.float32)
        grad_q = jnp.einsum('hts,sha->tha', grad_scores, key_wide) + jnp.einsum('thc,hac->tha', grad_wide, before_wide)
        grad_k = jnp.einsum('hts,tha->sha', grad_scores, query_wide) + jnp.einsum('shc,hac->sha', value_wide, beyond_wide)
        grad_v = jnp.einsum('hts,thc->shc', scores, grad_wide) + jnp.einsum('sha,hac->shc', key_wide, beyond_wide)
        return (grad_q.astype(jnp.bfloat16), grad_k.astype(jnp.bfloat16), grad_v.astype(jnp.bfloat16))
    grad_q, grad_k, grad_v = lax.map(backward_block, (query_blocks, key_blocks, value_blocks, grad_att_blocks, before, beyond))
    return (normed.reshape(SEQ, columns), grad_q.reshape(SEQ, columns), grad_k.reshape(SEQ, columns), grad_v.reshape(SEQ, columns))
```

```python
import jax
import jax.numpy as jnp
from jax import lax
from jax.experimental import pallas as pl
from jax.experimental.pallas import tpu as pltpu
from jax.sharding import Mesh, PartitionSpec as P

HEADS = 32
DH = 128
ROWS = 128
LOCAL = 8
HALF = LOCAL // 2
WIDTH = LOCAL * DH
WIDTH_ALL = HEADS * DH
EPSILON = 1e-06
X, Z, CORES, GROUPS = 4, 16, 2, 4
CHIPS = X * Z
PIECE = HALF * DH // CHIPS
F32 = jnp.float32
BF16 = jnp.bfloat16

VMEM = pl.BlockSpec(memory_space=pltpu.VMEM)
SMEM = pl.BlockSpec(memory_space=pltpu.SMEM)


def dot(a, b, ca, cb):
    return lax.dot_general(a, b, (((ca,), (cb,)), ((), ())), preferred_element_type=F32)


def head(ref, h):
    return ref[:, h * DH : (h + 1) * DH]


def causal():
    t = lax.broadcasted_iota(jnp.int32, (ROWS, ROWS), 0)
    s = lax.broadcasted_iota(jnp.int32, (ROWS, ROWS), 1)
    return s <= t


def call(kernel, shapes, flops, moved, specs):
    return pl.pallas_call(
        kernel,
        out_shape=[jax.ShapeDtypeStruct(s, d) for s, d in shapes],
        in_specs=specs,
        out_specs=[VMEM] * len(shapes),
        compiler_params=pltpu.CompilerParams(vmem_limit_bytes=32 * 1024 * 1024),
        cost_estimate=pl.CostEstimate(flops=flops, bytes_accessed=moved, transcendentals=0),
    )


MATMUL = LOCAL * 2 * DH * DH * DH
BLOCK = ROWS * WIDTH * 2


def states_kernel(k_ref, v_ref, s_ref, sent_ref):
    for h in range(LOCAL):
        state = dot(head(k_ref, h), head(v_ref, h), 0, 0)
        s_ref[h] = state
        sent_ref[h] = state.astype(BF16)


def pair_kernel(core_ref, own_ref, pair_ref, out_ref):
    other = 1 - core_ref[0]
    half = core_ref[0] * HALF
    for h in range(HALF):
        out_ref[h * DH : (h + 1) * DH, :] = (own_ref[half + h] + pair_ref[other, half + h].astype(F32)).astype(BF16)


def prefix_kernel(in_ref, out_ref):
    total = jnp.zeros((PIECE, DH), F32)
    for i in range(CHIPS // 2):
        two = in_ref[i * 2 * PIECE : (i + 1) * 2 * PIECE, :].astype(F32)
        middle = total + two[:PIECE]
        out_ref[i * 2 * PIECE : (i + 1) * 2 * PIECE, :] = jnp.concatenate([total, middle], axis=0).astype(BF16)
        total = middle + two[PIECE:]


def suffix_kernel(in_ref, out_ref):
    total = jnp.zeros((PIECE, DH), F32)
    for i in reversed(range(CHIPS // 2)):
        two = in_ref[i * 2 * PIECE : (i + 1) * 2 * PIECE, :].astype(F32)
        middle = total + two[PIECE:]
        out_ref[i * 2 * PIECE : (i + 1) * 2 * PIECE, :] = jnp.concatenate([middle, total], axis=0).astype(BF16)
        total = middle + two[:PIECE]


def inside_kernel(q_ref, k_ref, v_ref, scores_ref, inside_ref):
    mask = causal()
    for h in range(LOCAL):
        raw = dot(head(q_ref, h), head(k_ref, h), 1, 1)
        scores = jnp.where(mask, raw, 0.0).astype(BF16)
        scores_ref[h] = scores
        inside_ref[:, h * DH : (h + 1) * DH] = dot(scores, head(v_ref, h), 1, 0)


def attended_kernel(core_ref, q_ref, inside_ref, chips_ref, pair_ref, c_ref, gain_ref, att_ref, before_ref, sums_ref):
    second = core_ref[0] == 1
    squares = jnp.zeros((ROWS, DH), F32)
    crossed = jnp.zeros((ROWS, DH), F32)
    for h in range(LOCAL):
        other = jnp.where(second, pair_ref[0, h].astype(F32), 0.0)
        before = (chips_ref[h * DH : (h + 1) * DH, :].astype(F32) + other).astype(BF16)
        before_ref[h] = before
        att = head(inside_ref, h) + dot(head(q_ref, h), before, 1, 0)
        att_ref[:, h * DH : (h + 1) * DH] = att
        weighted = head(c_ref, h).astype(F32) * gain_ref[:, h * DH : (h + 1) * DH]
        squares = squares + att * att
        crossed = crossed + weighted * att
    row0 = jnp.sum(squares.T, axis=0, keepdims=True)
    row1 = jnp.sum(crossed.T, axis=0, keepdims=True)
    block = jnp.concatenate([row0, row1, jnp.zeros((6, ROWS), F32)], axis=0)
    for i in range(GROUPS):
        sums_ref[i * 8 : (i + 1) * 8, :] = block


def grad_kernel(sums_ref, att_ref, q_ref, c_ref, gain_ref, normed_ref, g_ref, products_ref, sent_ref):
    sums = sums_ref[0:8, :]
    for i in range(1, GROUPS):
        sums = sums + sums_ref[i * 8 : (i + 1) * 8, :]
    inverse_row = lax.rsqrt(sums[0:1] / WIDTH_ALL + EPSILON)
    cubed_row = inverse_row * inverse_row * inverse_row * (sums[1:2] / WIDTH_ALL)
    inverse = jnp.broadcast_to(inverse_row, (ROWS, ROWS)).T
    cubed = jnp.broadcast_to(cubed_row, (ROWS, ROWS)).T
    for h in range(LOCAL):
        at = slice(h * DH, (h + 1) * DH)
        att = att_ref[:, at]
        gain = gain_ref[:, at]
        normed_ref[:, at] = (att * inverse * gain).astype(BF16)
        weighted = c_ref[:, at].astype(F32) * gain
        g = (inverse * weighted - cubed * att).astype(BF16)
        g_ref[:, at] = g
        product = dot(q_ref[:, at], g, 0, 0)
        products_ref[h] = product
        sent_ref[h] = product.astype(BF16)


def local_grads_kernel(q_ref, k_ref, v_ref, g_ref, scores_ref, before_ref, gq_ref, gk_ref, gv_ref):
    mask = causal()
    for h in range(LOCAL):
        at = slice(h * DH, (h + 1) * DH)
        g = g_ref[:, at]
        raw = dot(g, v_ref[:, at], 1, 1)
        grad_scores = jnp.where(mask, raw, 0.0).astype(BF16)
        gq = dot(grad_scores, k_ref[:, at], 1, 0) + dot(g, before_ref[h], 1, 1)
        gq_ref[:, at] = gq.astype(BF16)
        gk_ref[:, at] = dot(grad_scores, q_ref[:, at], 0, 0)
        gv_ref[:, at] = dot(scores_ref[h], g, 0, 0)


def final_kernel(core_ref, k_ref, v_ref, gk_part_ref, gv_part_ref, chips_ref, pair_ref, gk_ref, gv_ref):
    first = core_ref[0] == 0
    for h in range(LOCAL):
        at = slice(h * DH, (h + 1) * DH)
        other = jnp.where(first, pair_ref[1, h].astype(F32), 0.0)
        beyond = (chips_ref[at, :].astype(F32) + other).astype(BF16)
        gk_ref[:, at] = (gk_part_ref[:, at] + dot(v_ref[:, at], beyond, 1, 1)).astype(BF16)
        gv_ref[:, at] = (gv_part_ref[:, at] + dot(k_ref[:, at], beyond, 1, 0)).astype(BF16)


STATE = (LOCAL, DH, DH)
FLAT = (HALF * DH, DH)


def chips_scan(core, own, pair, kernel):
    (mine,) = call(pair_kernel, [(FLAT, BF16)], 0, 4 * BLOCK, [SMEM, VMEM, VMEM])(core, own, pair)
    turned = lax.all_to_all(mine, ("x", "z"), 0, 0, tiled=True)
    (summed,) = call(kernel, [(FLAT, BF16)], 0, BLOCK, [VMEM])(turned)
    back = lax.all_to_all(summed, ("x", "z"), 0, 0, tiled=True)
    return lax.all_gather(back, "core", axis=0, tiled=True)


def local(q, k, v, gain, c):
    core = lax.axis_index("core").reshape(1).astype(jnp.int32)
    gain = gain.reshape(1, WIDTH)
    states, sent = call(states_kernel, [(STATE, F32), (STATE, BF16)], MATMUL, 5 * BLOCK, [VMEM] * 2)(k, v)
    pair = lax.all_gather(sent, "core")
    scores, inside = call(
        inside_kernel, [(STATE, BF16), ((ROWS, WIDTH), F32)], 2 * MATMUL, 6 * BLOCK, [VMEM] * 3
    )(q, k, v)
    chips = chips_scan(core, states, pair, prefix_kernel)
    att, before, sums = call(
        attended_kernel,
        [((ROWS, WIDTH), F32), (STATE, BF16), ((GROUPS * 8, ROWS), F32)],
        MATMUL, 10 * BLOCK, [SMEM] + [VMEM] * 6,
    )(core, q, inside, chips, pair, c, gain)
    sums = lax.all_to_all(sums, "head", 0, 0, tiled=True)
    normed, g, products, sent2 = call(
        grad_kernel,
        [((ROWS, WIDTH), BF16), ((ROWS, WIDTH), BF16), (STATE, F32), (STATE, BF16)],
        MATMUL, 10 * BLOCK, [VMEM] * 5,
    )(sums, att, q, c, gain)
    pair2 = lax.all_gather(sent2, "core")
    gq, gk_part, gv_part = call(
        local_grads_kernel,
        [((ROWS, WIDTH), BF16), ((ROWS, WIDTH), F32), ((ROWS, WIDTH), F32)],
        5 * MATMUL, 11 * BLOCK, [VMEM] * 6,
    )(q, k, v, g, scores, before)
    chips2 = chips_scan(core, products, pair2, suffix_kernel)
    gk, gv = call(
        final_kernel, [((ROWS, WIDTH), BF16), ((ROWS, WIDTH), BF16)], 2 * MATMUL, 12 * BLOCK, [SMEM] + [VMEM] * 6
    )(core, k, v, gk_part, gv_part, chips2, pair2)
    return normed, gq, gk, gv


def solution(mesh):
    fine = Mesh(mesh.devices.reshape(X, Z, CORES, GROUPS), ("x", "z", "core", "head"))
    block = P(("x", "z", "core"), "head")
    return jax.shard_map(
        local, mesh=fine, in_specs=(block, block, block, P("head"), block), out_specs=(block,) * 4, check_vma=False
    )
```

```python
import functools

import jax
import jax.numpy as jnp
from jax import lax
from jax.experimental import pallas as pl
from jax.experimental.pallas import tpu as pltpu
from jax.sharding import Mesh, PartitionSpec as P

HEADS = 32
DH = 128
ROWS = 128
LOCAL = 8
HALF = LOCAL // 2
WIDTH = LOCAL * DH
WIDTH_ALL = HEADS * DH
EPSILON = 1e-06
X, ZH, ZL, CORES, GROUPS = 4, 4, 4, 2, 4
PIECE = HALF * DH // (X * ZL)
F32 = jnp.float32
BF16 = jnp.bfloat16

VMEM = pl.BlockSpec(memory_space=pltpu.VMEM)
SMEM = pl.BlockSpec(memory_space=pltpu.SMEM)


def dot(a, b, ca, cb):
    return lax.dot_general(a, b, (((ca,), (cb,)), ((), ())), preferred_element_type=F32)


def head(ref, h):
    return ref[:, h * DH : (h + 1) * DH]


def causal():
    t = lax.broadcasted_iota(jnp.int32, (ROWS, ROWS), 0)
    s = lax.broadcasted_iota(jnp.int32, (ROWS, ROWS), 1)
    return s <= t


def call(kernel, shapes, flops, moved, specs):
    return pl.pallas_call(
        kernel,
        out_shape=[jax.ShapeDtypeStruct(s, d) for s, d in shapes],
        in_specs=specs,
        out_specs=[VMEM] * len(shapes),
        compiler_params=pltpu.CompilerParams(vmem_limit_bytes=32 * 1024 * 1024),
        cost_estimate=pl.CostEstimate(flops=flops, bytes_accessed=moved, transcendentals=0),
    )


MATMUL = LOCAL * 2 * DH * DH * DH
BLOCK = ROWS * WIDTH * 2


def states_kernel(k_ref, v_ref, s_ref, sent_ref):
    for h in range(LOCAL):
        state = dot(head(k_ref, h), head(v_ref, h), 0, 0)
        s_ref[h] = state
        sent_ref[h] = state.astype(BF16)


def pair_kernel(core_ref, own_ref, pair_ref, out_ref):
    other = 1 - core_ref[0]
    half = core_ref[0] * HALF
    for h in range(HALF):
        out_ref[h * DH : (h + 1) * DH, :] = (own_ref[half + h] + pair_ref[other, half + h].astype(F32)).astype(BF16)


def piece(ref, i):
    return ref[i * PIECE : (i + 1) * PIECE, :].astype(F32)


def cube_kernel(in_ref, out_ref):
    for x in range(X):
        total = piece(in_ref, x * ZL)
        for z in range(1, ZL):
            total = total + piece(in_ref, x * ZL + z)
        total = total.astype(BF16)
        for copy in range(ZH):
            at = (copy * X + x) * PIECE
            out_ref[at : at + PIECE, :] = total


def scan_kernel(reverse, place_ref, in_ref, cubes_ref, out_ref):
    here = place_ref[0]
    order = (lambda n: reversed(range(n))) if reverse else range
    column = jnp.zeros((PIECE, DH), F32)
    for x in order(X):
        total = column
        for z in range(ZH):
            cube = piece(cubes_ref, z * X + x)
            column = column + cube
            ahead = here < z if reverse else here > z
            total = total + jnp.where(ahead, cube, 0.0)
        for z in order(ZL):
            at = (x * ZL + z) * PIECE
            out_ref[at : at + PIECE, :] = total.astype(BF16)
            total = total + piece(in_ref, x * ZL + z)


def inside_kernel(q_ref, k_ref, v_ref, scores_ref, inside_ref):
    mask = causal()
    for h in range(LOCAL):
        raw = dot(head(q_ref, h), head(k_ref, h), 1, 1)
        scores = jnp.where(mask, raw, 0.0).astype(BF16)
        scores_ref[h] = scores
        inside_ref[:, h * DH : (h + 1) * DH] = dot(scores, head(v_ref, h), 1, 0)


def attended_kernel(core_ref, q_ref, inside_ref, chips_ref, pair_ref, c_ref, gain_ref, att_ref, before_ref, sums_ref):
    second = core_ref[0] == 1
    squares = jnp.zeros((ROWS, DH), F32)
    crossed = jnp.zeros((ROWS, DH), F32)
    for h in range(LOCAL):
        other = jnp.where(second, pair_ref[0, h].astype(F32), 0.0)
        before = (chips_ref[h * DH : (h + 1) * DH, :].astype(F32) + other).astype(BF16)
        before_ref[h] = before
        att = head(inside_ref, h) + dot(head(q_ref, h), before, 1, 0)
        att_ref[:, h * DH : (h + 1) * DH] = att
        weighted = head(c_ref, h).astype(F32) * gain_ref[:, h * DH : (h + 1) * DH]
        squares = squares + att * att
        crossed = crossed + weighted * att
    row0 = jnp.sum(squares.T, axis=0, keepdims=True)
    row1 = jnp.sum(crossed.T, axis=0, keepdims=True)
    block = jnp.concatenate([row0, row1, jnp.zeros((6, ROWS), F32)], axis=0)
    for i in range(GROUPS):
        sums_ref[i * 8 : (i + 1) * 8, :] = block


def grad_kernel(sums_ref, att_ref, q_ref, c_ref, gain_ref, normed_ref, g_ref, products_ref, sent_ref):
    sums = sums_ref[0:8, :]
    for i in range(1, GROUPS):
        sums = sums + sums_ref[i * 8 : (i + 1) * 8, :]
    inverse_row = lax.rsqrt(sums[0:1] / WIDTH_ALL + EPSILON)
    cubed_row = inverse_row * inverse_row * inverse_row * (sums[1:2] / WIDTH_ALL)
    inverse = jnp.broadcast_to(inverse_row, (ROWS, ROWS)).T
    cubed = jnp.broadcast_to(cubed_row, (ROWS, ROWS)).T
    for h in range(LOCAL):
        at = slice(h * DH, (h + 1) * DH)
        att = att_ref[:, at]
        gain = gain_ref[:, at]
        normed_ref[:, at] = (att * inverse * gain).astype(BF16)
        weighted = c_ref[:, at].astype(F32) * gain
        g = (inverse * weighted - cubed * att).astype(BF16)
        g_ref[:, at] = g
        product = dot(q_ref[:, at], g, 0, 0)
        products_ref[h] = product
        sent_ref[h] = product.astype(BF16)


def local_grads_kernel(q_ref, k_ref, v_ref, g_ref, scores_ref, before_ref, gq_ref, gk_ref, gv_ref):
    mask = causal()
    for h in range(LOCAL):
        at = slice(h * DH, (h + 1) * DH)
        g = g_ref[:, at]
        raw = dot(g, v_ref[:, at], 1, 1)
        grad_scores = jnp.where(mask, raw, 0.0).astype(BF16)
        gq = dot(grad_scores, k_ref[:, at], 1, 0) + dot(g, before_ref[h], 1, 1)
        gq_ref[:, at] = gq.astype(BF16)
        gk_ref[:, at] = dot(grad_scores, q_ref[:, at], 0, 0)
        gv_ref[:, at] = dot(scores_ref[h], g, 0, 0)


def final_kernel(core_ref, k_ref, v_ref, gk_part_ref, gv_part_ref, chips_ref, pair_ref, gk_ref, gv_ref):
    first = core_ref[0] == 0
    for h in range(LOCAL):
        at = slice(h * DH, (h + 1) * DH)
        other = jnp.where(first, pair_ref[1, h].astype(F32), 0.0)
        beyond = (chips_ref[at, :].astype(F32) + other).astype(BF16)
        gk_ref[:, at] = (gk_part_ref[:, at] + dot(v_ref[:, at], beyond, 1, 1)).astype(BF16)
        gv_ref[:, at] = (gv_part_ref[:, at] + dot(k_ref[:, at], beyond, 1, 0)).astype(BF16)


STATE = (LOCAL, DH, DH)
FLAT = (HALF * DH, DH)


def chips_scan(core, own, pair, reverse):
    (mine,) = call(pair_kernel, [(FLAT, BF16)], 0, 4 * BLOCK, [SMEM, VMEM, VMEM])(core, own, pair)
    place = lax.axis_index("zh").reshape(1).astype(jnp.int32)
    turned = lax.all_to_all(mine, ("x", "zl"), 0, 0, tiled=True)
    (cube,) = call(cube_kernel, [(FLAT, BF16)], 0, BLOCK, [VMEM])(turned)
    cubes = lax.all_to_all(cube, "zh", 0, 0, tiled=True)
    scan = functools.partial(scan_kernel, reverse)
    (summed,) = call(scan, [(FLAT, BF16)], 0, 2 * BLOCK, [SMEM, VMEM, VMEM])(place, turned, cubes)
    back = lax.all_to_all(summed, ("x", "zl"), 0, 0, tiled=True)
    return lax.all_gather(back, "core", axis=0, tiled=True)


def local(q, k, v, gain, c):
    core = lax.axis_index("core").reshape(1).astype(jnp.int32)
    gain = gain.reshape(1, WIDTH)
    states, sent = call(states_kernel, [(STATE, F32), (STATE, BF16)], MATMUL, 5 * BLOCK, [VMEM] * 2)(k, v)
    pair = lax.all_gather(sent, "core")
    scores, inside = call(
        inside_kernel, [(STATE, BF16), ((ROWS, WIDTH), F32)], 2 * MATMUL, 6 * BLOCK, [VMEM] * 3
    )(q, k, v)
    chips = chips_scan(core, states, pair, False)
    att, before, sums = call(
        attended_kernel,
        [((ROWS, WIDTH), F32), (STATE, BF16), ((GROUPS * 8, ROWS), F32)],
        MATMUL, 10 * BLOCK, [SMEM] + [VMEM] * 6,
    )(core, q, inside, chips, pair, c, gain)
    sums = lax.all_to_all(sums, "head", 0, 0, tiled=True)
    normed, g, products, sent2 = call(
        grad_kernel,
        [((ROWS, WIDTH), BF16), ((ROWS, WIDTH), BF16), (STATE, F32), (STATE, BF16)],
        MATMUL, 10 * BLOCK, [VMEM] * 5,
    )(sums, att, q, c, gain)
    pair2 = lax.all_gather(sent2, "core")
    gq, gk_part, gv_part = call(
        local_grads_kernel,
        [((ROWS, WIDTH), BF16), ((ROWS, WIDTH), F32), ((ROWS, WIDTH), F32)],
        5 * MATMUL, 11 * BLOCK, [VMEM] * 6,
    )(q, k, v, g, scores, before)
    chips2 = chips_scan(core, products, pair2, True)
    gk, gv = call(
        final_kernel, [((ROWS, WIDTH), BF16), ((ROWS, WIDTH), BF16)], 2 * MATMUL, 12 * BLOCK, [SMEM] + [VMEM] * 6
    )(core, k, v, gk_part, gv_part, chips2, pair2)
    return normed, gq, gk, gv


def solution(mesh):
    fine = Mesh(mesh.devices.reshape(X, ZH, ZL, CORES, GROUPS), ("x", "zh", "zl", "core", "head"))
    block = P(("x", "zh", "zl", "core"), "head")
    return jax.shard_map(
        local, mesh=fine, in_specs=(block, block, block, P("head"), block), out_specs=(block,) * 4, check_vma=False
    )
```

```python
import functools

import jax
import jax.numpy as jnp
from jax import lax
from jax.experimental import pallas as pl
from jax.experimental.pallas import tpu as pltpu
from jax.sharding import Mesh, PartitionSpec as P

HEADS = 32
DH = 128
ROWS = 128
X, ZH, ZL, CORES, GROUPS = 4, 4, 4, 2, 4
LOCAL = HEADS // GROUPS
HALF = LOCAL // CORES
CHUNK = CORES * ROWS
WIDTH = LOCAL * DH
PART = HALF * DH
WIDTH_ALL = HEADS * DH
EPSILON = 1e-06
PIECE = PART // (X * ZL)
X_ORDER = (2, 3, 0, 1)
ZL_ORDER = (3, 2, 1, 0)
ZH_ORDER = (2, 3, 0, 1)
PLANE = [[x * ZL + z for x in X_ORDER for z in ZL_ORDER]]
F32 = jnp.float32
BF16 = jnp.bfloat16

VMEM = pl.BlockSpec(memory_space=pltpu.VMEM)
SMEM = pl.BlockSpec(memory_space=pltpu.SMEM)


def dot(a, b, ca, cb):
    return lax.dot_general(a, b, (((ca,), (cb,)), ((), ())), preferred_element_type=F32)


def at(h):
    return slice(h * DH, (h + 1) * DH)


def wide(core_ref, ref, h):
    start = pl.multiple_of(core_ref[0] * PART, PART) + h * DH
    return ref[:, pl.ds(pl.multiple_of(start, DH), DH)]


def causal():
    t = lax.broadcasted_iota(jnp.int32, (CHUNK, CHUNK), 0)
    s = lax.broadcasted_iota(jnp.int32, (CHUNK, CHUNK), 1)
    return s <= t


def call(kernel, shapes, flops, moved, specs):
    return pl.pallas_call(
        kernel,
        out_shape=[jax.ShapeDtypeStruct(s, d) for s, d in shapes],
        in_specs=specs,
        out_specs=[VMEM] * len(shapes),
        compiler_params=pltpu.CompilerParams(vmem_limit_bytes=32 * 1024 * 1024),
        cost_estimate=pl.CostEstimate(flops=flops, bytes_accessed=moved, transcendentals=0),
    )


MATMUL = LOCAL * 2 * DH * DH * DH
BLOCK = ROWS * WIDTH * 2


def states_kernel(core_ref, k_ref, v_ref, mine_ref):
    for h in range(HALF):
        mine_ref[at(h), :] = dot(wide(core_ref, k_ref, h), wide(core_ref, v_ref, h), 0, 0).astype(BF16)


def spot(x, z):
    return (X_ORDER.index(x) * ZL + ZL_ORDER.index(z)) * PIECE


def piece(ref, start):
    return ref[start : start + PIECE, :].astype(F32)


def cube_kernel(in_ref, out_ref):
    for x in range(X):
        total = piece(in_ref, spot(x, 0))
        for z in range(1, ZL):
            total = total + piece(in_ref, spot(x, z))
        total = total.astype(BF16)
        for copy in range(ZH):
            start = (copy * X + x) * PIECE
            out_ref[start : start + PIECE, :] = total


def scan_kernel(reverse, place_ref, in_ref, cubes_ref, out_ref):
    here = place_ref[0]
    order = (lambda n: reversed(range(n))) if reverse else range
    column = jnp.zeros((PIECE, DH), F32)
    for x in order(X):
        total = column
        for z in range(ZH):
            cube = piece(cubes_ref, (ZH_ORDER.index(z) * X + x) * PIECE)
            column = column + cube
            ahead = here < z if reverse else here > z
            total = total + jnp.where(ahead, cube, 0.0)
        for z in order(ZL):
            start = spot(x, z)
            out_ref[start : start + PIECE, :] = total.astype(BF16)
            total = total + piece(in_ref, start)


def inside_kernel(core_ref, q_ref, k_ref, v_ref, scores_ref, inside_ref):
    mask = causal()
    for h in range(HALF):
        raw = dot(wide(core_ref, q_ref, h), wide(core_ref, k_ref, h), 1, 1)
        scores = jnp.where(mask, raw, 0.0).astype(BF16)
        scores_ref[h] = scores
        inside_ref[:, at(h)] = dot(scores, wide(core_ref, v_ref, h), 1, 0)


def rows_of(block):
    return [jnp.sum(block[i * ROWS : (i + 1) * ROWS].T, axis=0, keepdims=True) for i in range(CORES)]


def attended_kernel(core_ref, q_ref, inside_ref, before_ref, c_ref, gain_ref, att_ref, sums_ref):
    squares = jnp.zeros((CHUNK, DH), F32)
    crossed = jnp.zeros((CHUNK, DH), F32)
    for h in range(HALF):
        att = inside_ref[:, at(h)] + dot(wide(core_ref, q_ref, h), before_ref[at(h), :], 1, 0)
        att_ref[:, at(h)] = att
        weighted = wide(core_ref, c_ref, h).astype(F32) * wide(core_ref, gain_ref, h)
        squares = squares + att * att
        crossed = crossed + weighted * att
    block = jnp.concatenate(rows_of(squares) + rows_of(crossed) + [jnp.zeros((4, ROWS), F32)], axis=0)
    for i in range(CORES * GROUPS):
        sums_ref[i * 8 : (i + 1) * 8, :] = block


def tall(rows):
    return jnp.concatenate([jnp.broadcast_to(row, (ROWS, ROWS)).T for row in rows], axis=0)


def grad_kernel(core_ref, sums_ref, att_ref, q_ref, c_ref, gain_ref, normed_ref, g_ref, mine_ref):
    sums = sums_ref[0:8, :]
    for i in range(1, CORES * GROUPS):
        sums = sums + sums_ref[i * 8 : (i + 1) * 8, :]
    inverse_rows = lax.rsqrt(sums[0:2] / WIDTH_ALL + EPSILON)
    cubed_rows = inverse_rows * inverse_rows * inverse_rows * (sums[2:4] / WIDTH_ALL)
    inverse = tall([inverse_rows[0:1], inverse_rows[1:2]])
    cubed = tall([cubed_rows[0:1], cubed_rows[1:2]])
    for h in range(HALF):
        att = att_ref[:, at(h)]
        gain = wide(core_ref, gain_ref, h)
        normed_ref[:, at(h)] = (att * inverse * gain).astype(BF16)
        weighted = wide(core_ref, c_ref, h).astype(F32) * gain
        g = (inverse * weighted - cubed * att).astype(BF16)
        g_ref[:, at(h)] = g
        mine_ref[at(h), :] = dot(wide(core_ref, q_ref, h), g, 0, 0).astype(BF16)


def local_grads_kernel(core_ref, q_ref, k_ref, v_ref, g_ref, scores_ref, before_ref, gq_ref, gk_ref, gv_ref):
    mask = causal()
    for h in range(HALF):
        g = g_ref[:, at(h)]
        raw = dot(g, wide(core_ref, v_ref, h), 1, 1)
        grad_scores = jnp.where(mask, raw, 0.0).astype(BF16)
        gq = dot(grad_scores, wide(core_ref, k_ref, h), 1, 0) + dot(g, before_ref[at(h), :], 1, 1)
        gq_ref[:, at(h)] = gq.astype(BF16)
        gk_ref[:, at(h)] = dot(grad_scores, wide(core_ref, q_ref, h), 0, 0)
        gv_ref[:, at(h)] = dot(scores_ref[h], g, 0, 0)


def own_rows(core):
    return pl.ds(pl.multiple_of(core * ROWS, ROWS), ROWS)


def last_kernel(core_ref, k_ref, v_ref, gk_part_ref, gv_part_ref, beyond_ref, keep_ref, send_ref):
    core = core_ref[0]
    for h in range(HALF):
        column = pl.ds(pl.multiple_of(core * PART + h * DH, DH), DH)
        beyond = beyond_ref[at(h), :]
        for out_ref, rows in ((keep_ref, own_rows(core)), (send_ref, own_rows(1 - core))):
            gk = gk_part_ref[rows, at(h)] + dot(v_ref[rows, column], beyond, 1, 1)
            gv = gv_part_ref[rows, at(h)] + dot(k_ref[rows, column], beyond, 1, 0)
            out_ref[0:ROWS, at(h)] = gk.astype(BF16)
            out_ref[ROWS : 2 * ROWS, at(h)] = gv.astype(BF16)


def join_kernel(core_ref, keep_ref, got_ref, first_ref, second_ref):
    mine = pl.ds(pl.multiple_of(core_ref[0] * PART, PART), PART)
    other = pl.ds(pl.multiple_of((1 - core_ref[0]) * PART, PART), PART)
    for i, out_ref in enumerate((first_ref, second_ref)):
        rows = slice(i * ROWS, (i + 1) * ROWS)
        out_ref[:, mine] = keep_ref[rows, :]
        out_ref[:, other] = got_ref[rows, :]


def pick_kernel(core_ref, all_ref, out_ref):
    for i in range(CORES):
        rows = pl.ds(pl.multiple_of(i * CHUNK + core_ref[0] * ROWS, ROWS), ROWS)
        out_ref[:, i * PART : (i + 1) * PART] = all_ref[rows, :]


FLAT = (PART, DH)
TALL = (CHUNK, PART)
SCORES = (HALF, CHUNK, CHUNK)
OUT = (ROWS, WIDTH)


def plane_swap(a):
    return lax.all_to_all(a, ("x", "zl"), 0, 0, axis_index_groups=PLANE, tiled=True)


def chips_scan(mine, reverse, beside_turn=lambda: None, beside_cubes=lambda: None):
    place = lax.axis_index("zh").reshape(1).astype(jnp.int32)
    turned = plane_swap(mine)
    (cube,) = call(cube_kernel, [(FLAT, BF16)], 0, BLOCK, [VMEM])(turned)
    cube, extra = lax.optimization_barrier((cube, beside_turn()))
    cubes = lax.all_to_all(cube, "zh", 0, 0, axis_index_groups=[list(ZH_ORDER)], tiled=True)
    scan = functools.partial(scan_kernel, reverse)
    (summed,) = call(scan, [(FLAT, BF16)], 0, 2 * BLOCK, [SMEM, VMEM, VMEM])(place, turned, cubes)
    summed, more = lax.optimization_barrier((summed, beside_cubes()))
    return plane_swap(summed), extra, more


def pair(a):
    return lax.all_gather(a, "core", axis=0, tiled=True)


def picked(core, a):
    (out,) = call(pick_kernel, [(OUT, BF16)], 0, 3 * BLOCK, [SMEM, VMEM])(core, pair(a))
    return out


def local(q, k, v, gain, c):
    core = lax.axis_index("core").reshape(1).astype(jnp.int32)
    gain = gain.reshape(1, WIDTH)
    k, v, q, c = pair(k), pair(v), pair(q), pair(c)
    (mine,) = call(states_kernel, [(FLAT, BF16)], MATMUL, 5 * BLOCK, [SMEM] + [VMEM] * 2)(core, k, v)
    scores, inside = call(
        inside_kernel, [(SCORES, BF16), (TALL, F32)], 4 * MATMUL, 10 * BLOCK, [SMEM] + [VMEM] * 3
    )(core, q, k, v)
    before, _, _ = chips_scan(mine, False)
    att, sums = call(
        attended_kernel, [(TALL, F32), ((CORES * GROUPS * 8, ROWS), F32)], MATMUL, 10 * BLOCK, [SMEM] + [VMEM] * 5
    )(core, q, inside, before, c, gain)
    sums = lax.all_to_all(sums, ("core", "head"), 0, 0, tiled=True)
    normed, g, mine = call(
        grad_kernel, [(TALL, BF16), (TALL, BF16), (FLAT, BF16)], MATMUL, 9 * BLOCK, [SMEM] + [VMEM] * 5
    )(core, sums, att, q, c, gain)

    def grads():
        gq, gk_part, gv_part = call(
            local_grads_kernel, [(TALL, BF16), (TALL, F32), (TALL, F32)], 8 * MATMUL, 16 * BLOCK, [SMEM] + [VMEM] * 6
        )(core, q, k, v, g, scores, before)
        return picked(core, gq), gk_part, gv_part

    beyond, normed, (gq, gk_part, gv_part) = chips_scan(mine, True, lambda: picked(core, normed), grads)
    keep, send = call(last_kernel, [(TALL, BF16), (TALL, BF16)], 2 * MATMUL, 11 * BLOCK, [SMEM] + [VMEM] * 5)(
        core, k, v, gk_part, gv_part, beyond
    )
    got = lax.ppermute(send, "core", [(0, 1), (1, 0)])
    gk, gv = call(join_kernel, [(OUT, BF16), (OUT, BF16)], 0, 4 * BLOCK, [SMEM, VMEM, VMEM])(core, keep, got)
    return normed, gq, gk, gv


def solution(mesh):
    fine = Mesh(mesh.devices.reshape(X, ZH, ZL, CORES, GROUPS), ("x", "zh", "zl", "core", "head"))
    block = P(("x", "zh", "zl", "core"), "head")
    return jax.shard_map(
        local, mesh=fine, in_specs=(block, block, block, P("head"), block), out_specs=(block,) * 4, check_vma=False
    )
```

```python
import functools

import jax
import jax.numpy as jnp
from jax import lax
from jax.experimental import pallas as pl
from jax.experimental.pallas import tpu as pltpu
from jax.sharding import Mesh, PartitionSpec as P

HEADS = 32
DH = 128
ROWS = 128
X, ZH, ZL, CORES, GROUPS = 4, 4, 4, 2, 4
LOCAL = HEADS // GROUPS
HALF = LOCAL // CORES
CHUNK = CORES * ROWS
WIDTH = LOCAL * DH
PART = HALF * DH
WIDTH_ALL = HEADS * DH
EPSILON = 1e-06
PIECE = PART // (X * ZL)
X_ORDER = (2, 3, 0, 1)
ZL_ORDER = (2, 1, 3, 0)
ZH_ORDER = (2, 1, 3, 0)
PLANE = [[x * ZL + z for x in X_ORDER for z in ZL_ORDER]]
F32 = jnp.float32
BF16 = jnp.bfloat16

VMEM = pl.BlockSpec(memory_space=pltpu.VMEM)
SMEM = pl.BlockSpec(memory_space=pltpu.SMEM)


def dot(a, b, ca, cb):
    return lax.dot_general(a, b, (((ca,), (cb,)), ((), ())), preferred_element_type=F32)


def at(h):
    return slice(h * DH, (h + 1) * DH)


def wide(core_ref, ref, h):
    start = pl.multiple_of(core_ref[0] * PART, PART) + h * DH
    return ref[:, pl.ds(pl.multiple_of(start, DH), DH)]


def causal():
    t = lax.broadcasted_iota(jnp.int32, (CHUNK, CHUNK), 0)
    s = lax.broadcasted_iota(jnp.int32, (CHUNK, CHUNK), 1)
    return s <= t


def call(kernel, shapes, flops, moved, specs):
    return pl.pallas_call(
        kernel,
        out_shape=[jax.ShapeDtypeStruct(s, d) for s, d in shapes],
        in_specs=specs,
        out_specs=[VMEM] * len(shapes),
        compiler_params=pltpu.CompilerParams(vmem_limit_bytes=32 * 1024 * 1024),
        cost_estimate=pl.CostEstimate(flops=flops, bytes_accessed=moved, transcendentals=0),
    )


MATMUL = LOCAL * 2 * DH * DH * DH
BLOCK = ROWS * WIDTH * 2


def states_kernel(core_ref, k_ref, v_ref, mine_ref):
    for h in range(HALF):
        mine_ref[at(h), :] = dot(wide(core_ref, k_ref, h), wide(core_ref, v_ref, h), 0, 0).astype(BF16)


def spot(x, z):
    return (X_ORDER.index(x) * ZL + ZL_ORDER.index(z)) * PIECE


def piece(ref, start):
    return ref[start : start + PIECE, :].astype(F32)


def cube_kernel(in_ref, out_ref):
    for x in range(X):
        total = piece(in_ref, spot(x, 0))
        for z in range(1, ZL):
            total = total + piece(in_ref, spot(x, z))
        total = total.astype(BF16)
        for copy in range(ZH):
            start = (copy * X + x) * PIECE
            out_ref[start : start + PIECE, :] = total


def scan_kernel(reverse, place_ref, in_ref, cubes_ref, out_ref):
    here = place_ref[0]
    order = (lambda n: reversed(range(n))) if reverse else range
    column = jnp.zeros((PIECE, DH), F32)
    for x in order(X):
        total = column
        for z in range(ZH):
            cube = piece(cubes_ref, (ZH_ORDER.index(z) * X + x) * PIECE)
            column = column + cube
            ahead = here < z if reverse else here > z
            total = total + jnp.where(ahead, cube, 0.0)
        for z in order(ZL):
            start = spot(x, z)
            out_ref[start : start + PIECE, :] = total.astype(BF16)
            total = total + piece(in_ref, start)


def inside_kernel(core_ref, q_ref, k_ref, v_ref, c_ref, gain_ref, inside_ref, weighted_ref, near_gain_ref):
    mask = causal()
    for h in range(HALF):
        raw = dot(wide(core_ref, q_ref, h), wide(core_ref, k_ref, h), 1, 1)
        scores = jnp.where(mask, raw, 0.0).astype(BF16)
        inside_ref[:, at(h)] = dot(scores, wide(core_ref, v_ref, h), 1, 0)
        gain = wide(core_ref, gain_ref, h)
        near_gain_ref[:, at(h)] = jnp.broadcast_to(gain, (8, DH))
        weighted_ref[:, at(h)] = wide(core_ref, c_ref, h).astype(F32) * gain


def rows_of(block):
    return [jnp.sum(block[i * ROWS : (i + 1) * ROWS].T, axis=0, keepdims=True) for i in range(CORES)]


def attended_kernel(core_ref, q_ref, inside_ref, before_ref, weighted_ref, att_ref, sums_ref):
    squares = jnp.zeros((CHUNK, DH), F32)
    crossed = jnp.zeros((CHUNK, DH), F32)
    for h in range(HALF):
        att = inside_ref[:, at(h)] + dot(wide(core_ref, q_ref, h), before_ref[at(h), :], 1, 0)
        att_ref[:, at(h)] = att
        squares = squares + att * att
        crossed = crossed + weighted_ref[:, at(h)] * att
    block = jnp.concatenate(rows_of(squares) + rows_of(crossed) + [jnp.zeros((4, ROWS), F32)], axis=0)
    for i in range(CORES * GROUPS):
        sums_ref[i * 8 : (i + 1) * 8, :] = block


def tall(rows):
    return jnp.concatenate([jnp.broadcast_to(row, (ROWS, ROWS)).T for row in rows], axis=0)


def grad_kernel(core_ref, sums_ref, att_ref, q_ref, weighted_ref, gain_ref, normed_ref, g_ref, mine_ref):
    sums = sums_ref[0:8, :]
    for i in range(1, CORES * GROUPS):
        sums = sums + sums_ref[i * 8 : (i + 1) * 8, :]
    inverse_rows = lax.rsqrt(sums[0:2] / WIDTH_ALL + EPSILON)
    cubed_rows = inverse_rows * inverse_rows * inverse_rows * (sums[2:4] / WIDTH_ALL)
    inverse = tall([inverse_rows[0:1], inverse_rows[1:2]])
    cubed = tall([cubed_rows[0:1], cubed_rows[1:2]])
    for h in range(HALF):
        att = att_ref[:, at(h)]
        normed_ref[:, at(h)] = (att * inverse * gain_ref[0:1, at(h)]).astype(BF16)
        g = (inverse * weighted_ref[:, at(h)] - cubed * att).astype(BF16)
        g_ref[:, at(h)] = g
        mine_ref[at(h), :] = dot(wide(core_ref, q_ref, h), g, 0, 0).astype(BF16)


def own_rows(core):
    return pl.ds(pl.multiple_of(core * ROWS, ROWS), ROWS)


def local_grads_kernel(
    core_ref, q_ref, k_ref, v_ref, g_ref, before_ref, normed_ref, keep_ref, send_ref, gk_ref, gv_ref, gq_ref
):
    mask = causal()
    for h in range(HALF):
        q, k, v, g = wide(core_ref, q_ref, h), wide(core_ref, k_ref, h), wide(core_ref, v_ref, h), g_ref[:, at(h)]
        scores = jnp.where(mask, dot(q, k, 1, 1), 0.0).astype(BF16)
        grad_scores = jnp.where(mask, dot(g, v, 1, 1), 0.0).astype(BF16)
        gq_ref[:, at(h)] = (dot(grad_scores, k, 1, 0) + dot(g, before_ref[at(h), :], 1, 1)).astype(BF16)
        gk_ref[:, at(h)] = dot(grad_scores, q, 0, 0)
        gv_ref[:, at(h)] = dot(scores, g, 0, 0)
    for out_ref, rows in ((keep_ref, own_rows(core_ref[0])), (send_ref, own_rows(1 - core_ref[0]))):
        out_ref[0:ROWS, :] = normed_ref[rows, :]
        out_ref[ROWS : 2 * ROWS, :] = gq_ref[rows, :]


def last_kernel(core_ref, k_ref, v_ref, gk_part_ref, gv_part_ref, beyond_ref, keep_ref, send_ref):
    core = core_ref[0]
    for h in range(HALF):
        column = pl.ds(pl.multiple_of(core * PART + h * DH, DH), DH)
        beyond = beyond_ref[at(h), :]
        for out_ref, rows in ((keep_ref, own_rows(core)), (send_ref, own_rows(1 - core))):
            gk = gk_part_ref[rows, at(h)] + dot(v_ref[rows, column], beyond, 1, 1)
            gv = gv_part_ref[rows, at(h)] + dot(k_ref[rows, column], beyond, 1, 0)
            out_ref[0:ROWS, at(h)] = gk.astype(BF16)
            out_ref[ROWS : 2 * ROWS, at(h)] = gv.astype(BF16)


def join_kernel(core_ref, keep_ref, sent_ref, first_ref, second_ref):
    core, other = core_ref[0], 1 - core_ref[0]
    for i, out_ref in enumerate((first_ref, second_ref)):
        out_ref[:, pl.ds(pl.multiple_of(core * PART, PART), PART)] = keep_ref[i * ROWS : (i + 1) * ROWS, :]
        rows = pl.ds(pl.multiple_of(other * CHUNK + i * ROWS, ROWS), ROWS)
        out_ref[:, pl.ds(pl.multiple_of(other * PART, PART), PART)] = sent_ref[rows, :]


FLAT = (PART, DH)
TALL = (CHUNK, PART)
OUT = (ROWS, WIDTH)


def plane_swap(a):
    return lax.all_to_all(a, ("x", "zl"), 0, 0, axis_index_groups=PLANE, tiled=True)


def chips_scan(mine, reverse, beside_turn=lambda: None, beside_cubes=lambda: None):
    place = lax.axis_index("zh").reshape(1).astype(jnp.int32)
    turned = plane_swap(mine)
    (cube,) = call(cube_kernel, [(FLAT, BF16)], 0, BLOCK, [VMEM])(turned)
    cube, extra = lax.optimization_barrier((cube, beside_turn()))
    cubes = lax.all_to_all(cube, "zh", 0, 0, axis_index_groups=[list(ZH_ORDER)], tiled=True)
    scan = functools.partial(scan_kernel, reverse)
    (summed,) = call(scan, [(FLAT, BF16)], 0, 2 * BLOCK, [SMEM, VMEM, VMEM])(place, turned, cubes)
    summed, more = lax.optimization_barrier((summed, beside_cubes()))
    return plane_swap(summed), extra, more


def pair(a):
    return lax.all_gather(a, "core", axis=0, tiled=True)


def joined(core, keep, send):
    return call(join_kernel, [(OUT, BF16), (OUT, BF16)], 0, 4 * BLOCK, [SMEM, VMEM, VMEM])(core, keep, pair(send))


def local(q, k, v, gain, c):
    core = lax.axis_index("core").reshape(1).astype(jnp.int32)
    gain = gain.reshape(1, WIDTH)
    k, v = pair(k), pair(v)
    (mine,) = call(states_kernel, [(FLAT, BF16)], MATMUL, 5 * BLOCK, [SMEM] + [VMEM] * 2)(core, k, v)
    q, c = pair(q), pair(c)

    def prepare():
        return call(
            inside_kernel, [(TALL, F32), (TALL, F32), ((8, PART), F32)], 4 * MATMUL, 12 * BLOCK, [SMEM] + [VMEM] * 5
        )(core, q, k, v, c, gain)

    before, q, (inside, weighted, near_gain) = chips_scan(mine, False, lambda: q, prepare)
    att, sums = call(
        attended_kernel, [(TALL, F32), ((CORES * GROUPS * 8, ROWS), F32)], MATMUL, 10 * BLOCK, [SMEM] + [VMEM] * 4
    )(core, q, inside, before, weighted)
    sums = lax.all_to_all(sums, ("core", "head"), 0, 0, axis_index_groups=[[2, 6, 3, 7, 0, 4, 1, 5]], tiled=True)
    normed, g, mine = call(
        grad_kernel, [(TALL, BF16), (TALL, BF16), (FLAT, BF16)], MATMUL, 9 * BLOCK, [SMEM] + [VMEM] * 5
    )(core, sums, att, q, weighted, near_gain)
    keep, send, gk_part, gv_part, _ = call(
        local_grads_kernel,
        [(TALL, BF16), (TALL, BF16), (TALL, F32), (TALL, F32), (TALL, BF16)],
        12 * MATMUL, 18 * BLOCK, [SMEM] + [VMEM] * 6,
    )(core, q, k, v, g, before, normed)
    beyond, (gk_part, gv_part), (normed, gq) = chips_scan(
        mine, True, lambda: (gk_part, gv_part), lambda: joined(core, keep, send)
    )
    keep, send = call(last_kernel, [(TALL, BF16), (TALL, BF16)], 2 * MATMUL, 11 * BLOCK, [SMEM] + [VMEM] * 5)(
        core, k, v, gk_part, gv_part, beyond
    )
    gk, gv = joined(core, keep, send)
    return normed, gq, gk, gv


def solution(mesh):
    fine = Mesh(mesh.devices.reshape(X, ZH, ZL, CORES, GROUPS), ("x", "zh", "zl", "core", "head"))
    block = P(("x", "zh", "zl", "core"), "head")
    return jax.shard_map(
        local, mesh=fine, in_specs=(block, block, block, P("head"), block), out_specs=(block,) * 4, check_vma=False
    )
```

```python
import functools

import jax
import jax.numpy as jnp
from jax import lax
from jax.experimental import pallas as pl
from jax.experimental.pallas import tpu as pltpu
from jax.sharding import Mesh, PartitionSpec as P

HEADS = 32
DH = 128
ROWS = 128
X, ZH, ZL, CORES, GROUPS = 4, 4, 4, 2, 4
LOCAL = HEADS // GROUPS
HALF = LOCAL // CORES
CHUNK = CORES * ROWS
WIDTH = LOCAL * DH
PART = HALF * DH
WIDTH_ALL = HEADS * DH
EPSILON = 1e-06
PIECE = PART // (X * ZL)
X_ORDER = (2, 1, 3, 0)
ZL_ORDER = (2, 1, 3, 0)
ZH_ORDER = (2, 1, 3, 0)
SUM_ORDER = [2, 6, 3, 7, 0, 4, 1, 5]
PLANE = [[x * ZL + z for x in X_ORDER for z in ZL_ORDER]]
F32 = jnp.float32
BF16 = jnp.bfloat16

VMEM = pl.BlockSpec(memory_space=pltpu.VMEM)
SMEM = pl.BlockSpec(memory_space=pltpu.SMEM)
ANY = pl.BlockSpec(memory_space=pl.ANY)


def dot(a, b, ca, cb):
    return lax.dot_general(a, b, (((ca,), (cb,)), ((), ())), preferred_element_type=F32)


def at(h):
    return slice(h * DH, (h + 1) * DH)


def part_of(core, size):
    return pl.ds(pl.multiple_of(core * size, size), size)


def causal():
    t = lax.broadcasted_iota(jnp.int32, (CHUNK, CHUNK), 0)
    s = lax.broadcasted_iota(jnp.int32, (CHUNK, CHUNK), 1)
    return s <= t


def call(kernel, shapes, flops, moved, specs, scratch=(), out=VMEM):
    return pl.pallas_call(
        kernel,
        out_shape=[jax.ShapeDtypeStruct(s, d) for s, d in shapes],
        in_specs=specs,
        out_specs=[out] * len(shapes),
        scratch_shapes=scratch,
        compiler_params=pltpu.CompilerParams(vmem_limit_bytes=32 * 1024 * 1024),
        cost_estimate=pl.CostEstimate(flops=flops, bytes_accessed=moved, transcendentals=0),
    )


MATMUL = LOCAL * 2 * DH * DH * DH
BLOCK = ROWS * WIDTH * 2


def pack_kernel(core_ref, a_ref, b_ref, send_ref, sems):
    leaving = part_of(1 - core_ref[0], PART)
    copies = [
        pltpu.make_async_copy(ref.at[:, leaving], send_ref.at[pl.ds(i * ROWS, ROWS), :], sems.at[i])
        for i, ref in enumerate((a_ref, b_ref))
    ]
    for copy in copies:
        copy.start()
    for copy in copies:
        copy.wait()


def arrived(core, sent_ref, i):
    other = 1 - core
    return sent_ref[pl.ds(pl.multiple_of(other * CHUNK + i * ROWS, ROWS), ROWS), :]


def assemble(core, own_ref, sent_ref, i, near_ref):
    near_ref[part_of(core, ROWS), :] = own_ref[:, part_of(core, PART)]
    near_ref[part_of(1 - core, ROWS), :] = arrived(core, sent_ref, i)


def states_kernel(core_ref, k_ref, v_ref, sent_ref, k_near_ref, v_near_ref, mine_ref):
    assemble(core_ref[0], k_ref, sent_ref, 0, k_near_ref)
    assemble(core_ref[0], v_ref, sent_ref, 1, v_near_ref)
    for h in range(HALF):
        mine_ref[at(h), :] = dot(k_near_ref[:, at(h)], v_near_ref[:, at(h)], 0, 0).astype(BF16)


def spot(x, z):
    return (X_ORDER.index(x) * ZL + ZL_ORDER.index(z)) * PIECE


def piece(ref, start):
    return ref[start : start + PIECE, :].astype(F32)


def cube_kernel(in_ref, out_ref):
    for x in range(X):
        total = piece(in_ref, spot(x, 0))
        for z in range(1, ZL):
            total = total + piece(in_ref, spot(x, z))
        total = total.astype(BF16)
        for copy in range(ZH):
            start = (copy * X + x) * PIECE
            out_ref[start : start + PIECE, :] = total


def scan_kernel(reverse, place_ref, in_ref, cubes_ref, out_ref):
    here = place_ref[0]
    order = (lambda n: reversed(range(n))) if reverse else range
    column = jnp.zeros((PIECE, DH), F32)
    for x in order(X):
        total = column
        for z in range(ZH):
            cube = piece(cubes_ref, (ZH_ORDER.index(z) * X + x) * PIECE)
            column = column + cube
            ahead = here < z if reverse else here > z
            total = total + jnp.where(ahead, cube, 0.0)
        for z in order(ZL):
            start = spot(x, z)
            out_ref[start : start + PIECE, :] = total.astype(BF16)
            total = total + piece(in_ref, start)


def inside_kernel(
    core_ref, q_ref, c_ref, sent_ref, k_ref, v_ref, gain_ref, q_near_ref, inside_ref, weighted_ref, near_gain_ref
):
    core = core_ref[0]
    mask = causal()
    assemble(core, q_ref, sent_ref, 0, q_near_ref)
    gain = gain_ref[:, part_of(core, PART)]
    near_gain_ref[...] = jnp.broadcast_to(gain, (8, PART))
    weighted_ref[part_of(core, ROWS), :] = c_ref[:, part_of(core, PART)].astype(F32) * gain
    weighted_ref[part_of(1 - core, ROWS), :] = arrived(core, sent_ref, 1).astype(F32) * gain
    for h in range(HALF):
        raw = dot(q_near_ref[:, at(h)], k_ref[:, at(h)], 1, 1)
        scores = jnp.where(mask, raw, 0.0).astype(BF16)
        inside_ref[:, at(h)] = dot(scores, v_ref[:, at(h)], 1, 0)


def rows_of(block):
    return [jnp.sum(block[i * ROWS : (i + 1) * ROWS].T, axis=0, keepdims=True) for i in range(CORES)]


def attended_kernel(q_ref, inside_ref, before_ref, weighted_ref, att_ref, sums_ref):
    squares = jnp.zeros((CHUNK, DH), F32)
    crossed = jnp.zeros((CHUNK, DH), F32)
    for h in range(HALF):
        att = inside_ref[:, at(h)] + dot(q_ref[:, at(h)], before_ref[at(h), :], 1, 0)
        att_ref[:, at(h)] = att
        squares = squares + att * att
        crossed = crossed + weighted_ref[:, at(h)] * att
    block = jnp.concatenate(rows_of(squares) + rows_of(crossed) + [jnp.zeros((4, ROWS), F32)], axis=0)
    for i in range(CORES * GROUPS):
        sums_ref[i * 8 : (i + 1) * 8, :] = block


def tall(rows):
    return jnp.concatenate([jnp.broadcast_to(row, (ROWS, ROWS)).T for row in rows], axis=0)


def token_scales(sums_ref):
    sums = sums_ref[0:8, :]
    for i in range(1, CORES * GROUPS):
        sums = sums + sums_ref[i * 8 : (i + 1) * 8, :]
    inverse_rows = lax.rsqrt(sums[0:2] / WIDTH_ALL + EPSILON)
    cubed_rows = inverse_rows * inverse_rows * inverse_rows * (sums[2:4] / WIDTH_ALL)
    return tall([inverse_rows[0:1], inverse_rows[1:2]]), tall([cubed_rows[0:1], cubed_rows[1:2]])


def grad_of(inverse, cubed, weighted_ref, att_ref, h):
    return (inverse * weighted_ref[:, at(h)] - cubed * att_ref[:, at(h)]).astype(BF16)


def products_kernel(sums_ref, att_ref, q_ref, weighted_ref, mine_ref):
    inverse, cubed = token_scales(sums_ref)
    for h in range(HALF):
        g = grad_of(inverse, cubed, weighted_ref, att_ref, h)
        mine_ref[at(h), :] = dot(q_ref[:, at(h)], g, 0, 0).astype(BF16)


def local_grads_kernel(
    core_ref, sums_ref, att_ref, weighted_ref, gain_ref, q_ref, k_ref, v_ref, before_ref,
    keep_ref, send_ref, gk_ref, gv_ref, normed_ref, gq_ref,
):
    mask = causal()
    inverse, cubed = token_scales(sums_ref)
    for h in range(HALF):
        q, k, v = q_ref[:, at(h)], k_ref[:, at(h)], v_ref[:, at(h)]
        normed_ref[:, at(h)] = (att_ref[:, at(h)] * inverse * gain_ref[0:1, at(h)]).astype(BF16)
        g = grad_of(inverse, cubed, weighted_ref, att_ref, h)
        scores = jnp.where(mask, dot(q, k, 1, 1), 0.0).astype(BF16)
        grad_scores = jnp.where(mask, dot(g, v, 1, 1), 0.0).astype(BF16)
        gq_ref[:, at(h)] = (dot(grad_scores, k, 1, 0) + dot(g, before_ref[at(h), :], 1, 1)).astype(BF16)
        gk_ref[:, at(h)] = dot(grad_scores, q, 0, 0)
        gv_ref[:, at(h)] = dot(scores, g, 0, 0)
    for out_ref, core in ((keep_ref, core_ref[0]), (send_ref, 1 - core_ref[0])):
        out_ref[0:ROWS, :] = normed_ref[part_of(core, ROWS), :]
        out_ref[ROWS : 2 * ROWS, :] = gq_ref[part_of(core, ROWS), :]


def last_kernel(core_ref, k_ref, v_ref, gk_part_ref, gv_part_ref, beyond_ref, keep_ref, send_ref):
    for h in range(HALF):
        beyond = beyond_ref[at(h), :]
        for out_ref, core in ((keep_ref, core_ref[0]), (send_ref, 1 - core_ref[0])):
            rows = part_of(core, ROWS)
            gk = gk_part_ref[rows, at(h)] + dot(v_ref[rows, at(h)], beyond, 1, 1)
            gv = gv_part_ref[rows, at(h)] + dot(k_ref[rows, at(h)], beyond, 1, 0)
            out_ref[0:ROWS, at(h)] = gk.astype(BF16)
            out_ref[ROWS : 2 * ROWS, at(h)] = gv.astype(BF16)


def join_kernel(core_ref, keep_ref, sent_ref, first_ref, second_ref):
    core = core_ref[0]
    for i, out_ref in enumerate((first_ref, second_ref)):
        out_ref[:, part_of(core, PART)] = keep_ref[i * ROWS : (i + 1) * ROWS, :]
        out_ref[:, part_of(1 - core, PART)] = arrived(core, sent_ref, i)


FLAT = (PART, DH)
TALL = (CHUNK, PART)
OUT = (ROWS, WIDTH)


def plane_swap(a):
    return lax.all_to_all(a, ("x", "zl"), 0, 0, axis_index_groups=PLANE, tiled=True)


def chips_scan(mine, reverse, beside_turn=lambda: None, beside_cubes=lambda: None):
    place = lax.axis_index("zh").reshape(1).astype(jnp.int32)
    turned = plane_swap(mine)
    (cube,) = call(cube_kernel, [(FLAT, BF16)], 0, BLOCK, [VMEM])(turned)
    cube, extra = lax.optimization_barrier((cube, beside_turn()))
    cubes = lax.all_to_all(cube, "zh", 0, 0, axis_index_groups=[list(ZH_ORDER)], tiled=True)
    scan = functools.partial(scan_kernel, reverse)
    (summed,) = call(scan, [(FLAT, BF16)], 0, 2 * BLOCK, [SMEM, VMEM, VMEM])(place, turned, cubes)
    summed, more = lax.optimization_barrier((summed, beside_cubes()))
    return plane_swap(summed), extra, more


def pair(a):
    return lax.all_gather(a, "core", axis=0, tiled=True)


def joined(core, keep, send):
    return call(join_kernel, [(OUT, BF16), (OUT, BF16)], 0, 4 * BLOCK, [SMEM, VMEM, VMEM])(core, keep, pair(send))


def swapped(core, a, b):
    (send,) = call(
        pack_kernel, [(TALL, BF16)], 0, 2 * BLOCK, [SMEM, ANY, ANY], [pltpu.SemaphoreType.DMA((2,))], ANY
    )(core, a, b)
    return pair(send)


def local(q, k, v, gain, c):
    core = lax.axis_index("core").reshape(1).astype(jnp.int32)
    gain = gain.reshape(1, WIDTH)
    k, v, mine = call(
        states_kernel, [(TALL, BF16), (TALL, BF16), (FLAT, BF16)], MATMUL, 5 * BLOCK, [SMEM] + [VMEM] * 3
    )(core, k, v, swapped(core, k, v))
    sent = swapped(core, q, c)

    def prepare():
        return call(
            inside_kernel,
            [(TALL, BF16), (TALL, F32), (TALL, F32), ((8, PART), F32)],
            4 * MATMUL, 12 * BLOCK, [SMEM] + [VMEM] * 6,
        )(core, q, c, sent, k, v, gain)

    before, sent, (q_near, inside, weighted, near_gain) = chips_scan(mine, False, lambda: sent, prepare)
    att, sums = call(
        attended_kernel, [(TALL, F32), ((CORES * GROUPS * 8, ROWS), F32)], MATMUL, 10 * BLOCK, [VMEM] * 4
    )(q_near, inside, before, weighted)
    sums = lax.all_to_all(sums, ("core", "head"), 0, 0, axis_index_groups=[SUM_ORDER], tiled=True)
    (mine,) = call(products_kernel, [(FLAT, BF16)], MATMUL, 6 * BLOCK, [VMEM] * 4)(sums, att, q_near, weighted)
    keep, send, gk_part, gv_part = call(
        local_grads_kernel,
        [(TALL, BF16), (TALL, BF16), (TALL, F32), (TALL, F32)],
        12 * MATMUL, 18 * BLOCK, [SMEM] + [VMEM] * 8, [pltpu.VMEM(TALL, BF16)] * 2,
    )(core, sums, att, weighted, near_gain, q_near, k, v, before)
    beyond, (gk_part, gv_part), (normed, gq) = chips_scan(
        mine, True, lambda: (gk_part, gv_part), lambda: joined(core, keep, send)
    )
    keep, send = call(last_kernel, [(TALL, BF16), (TALL, BF16)], 2 * MATMUL, 11 * BLOCK, [SMEM] + [VMEM] * 5)(
        core, k, v, gk_part, gv_part, beyond
    )
    gk, gv = joined(core, keep, send)
    return normed, gq, gk, gv


def solution(mesh):
    fine = Mesh(mesh.devices.reshape(X, ZH, ZL, CORES, GROUPS), ("x", "zh", "zl", "core", "head"))
    block = P(("x", "zh", "zl", "core"), "head")
    return jax.shard_map(
        local, mesh=fine, in_specs=(block, block, block, P("head"), block), out_specs=(block,) * 4, check_vma=False
    )
```

```python
import functools

import jax
import jax.numpy as jnp
from jax import lax
from jax.experimental import pallas as pl
from jax.experimental.pallas import tpu as pltpu
from jax.sharding import Mesh, PartitionSpec as P

HEADS = 32
DH = 128
ROWS = 128
X, ZH, ZL, CORES, GROUPS = 4, 4, 4, 2, 4
LOCAL = HEADS // GROUPS
HALF = LOCAL // CORES
CHUNK = CORES * ROWS
WIDTH = LOCAL * DH
PART = HALF * DH
WIDTH_ALL = HEADS * DH
EPSILON = 1e-06
PIECE = PART // (X * ZL)
X_ORDER = (2, 1, 3, 0)
ZL_ORDER = (2, 1, 3, 0)
ZH_ORDER = (2, 1, 3, 0)
SUM_ORDER = [2, 6, 3, 7, 0, 4, 1, 5]
PLANE = [[x * ZL + z for x in X_ORDER for z in ZL_ORDER]]
F32 = jnp.float32
BF16 = jnp.bfloat16

VMEM = pl.BlockSpec(memory_space=pltpu.VMEM)
SMEM = pl.BlockSpec(memory_space=pltpu.SMEM)
ANY = pl.BlockSpec(memory_space=pl.ANY)


def dot(a, b, ca, cb):
    return lax.dot_general(a, b, (((ca,), (cb,)), ((), ())), preferred_element_type=F32)


def at(h):
    return slice(h * DH, (h + 1) * DH)


def part_of(core, size):
    return pl.ds(pl.multiple_of(core * size, size), size)


def causal():
    t = lax.broadcasted_iota(jnp.int32, (CHUNK, CHUNK), 0)
    s = lax.broadcasted_iota(jnp.int32, (CHUNK, CHUNK), 1)
    return s <= t


def call(kernel, shapes, flops, moved, specs, scratch=(), out=VMEM):
    return pl.pallas_call(
        kernel,
        out_shape=[jax.ShapeDtypeStruct(s, d) for s, d in shapes],
        in_specs=specs,
        out_specs=[out] * len(shapes),
        scratch_shapes=scratch,
        compiler_params=pltpu.CompilerParams(vmem_limit_bytes=32 * 1024 * 1024),
        cost_estimate=pl.CostEstimate(flops=flops, bytes_accessed=moved, transcendentals=0),
    )


MATMUL = LOCAL * 2 * DH * DH * DH
BLOCK = ROWS * WIDTH * 2


def pack_kernel(core_ref, a_ref, b_ref, send_ref, sems):
    leaving = part_of(1 - core_ref[0], PART)
    copies = [
        pltpu.make_async_copy(ref.at[:, leaving], send_ref.at[pl.ds(i * ROWS, ROWS), :], sems.at[i])
        for i, ref in enumerate((a_ref, b_ref))
    ]
    for copy in copies:
        copy.start()
    for copy in copies:
        copy.wait()


def arrived(core, sent_ref, i):
    other = 1 - core
    return sent_ref[pl.ds(pl.multiple_of(other * CHUNK + i * ROWS, ROWS), ROWS), :]


def assemble(core, own_ref, sent_ref, i, near_ref):
    near_ref[part_of(core, ROWS), :] = own_ref[:, part_of(core, PART)]
    near_ref[part_of(1 - core, ROWS), :] = arrived(core, sent_ref, i)


def states_kernel(core_ref, k_ref, v_ref, sent_ref, k_near_ref, v_near_ref, mine_ref):
    assemble(core_ref[0], k_ref, sent_ref, 0, k_near_ref)
    assemble(core_ref[0], v_ref, sent_ref, 1, v_near_ref)
    for h in range(HALF):
        mine_ref[at(h), :] = dot(k_near_ref[:, at(h)], v_near_ref[:, at(h)], 0, 0).astype(BF16)


def spot(x, z):
    return (X_ORDER.index(x) * ZL + ZL_ORDER.index(z)) * PIECE


def piece(ref, start):
    return ref[start : start + PIECE, :].astype(F32)


def cube_kernel(in_ref, out_ref):
    for x in range(X):
        total = piece(in_ref, spot(x, 0))
        for z in range(1, ZL):
            total = total + piece(in_ref, spot(x, z))
        total = total.astype(BF16)
        for copy in range(ZH):
            start = (copy * X + x) * PIECE
            out_ref[start : start + PIECE, :] = total


def scan_kernel(reverse, place_ref, in_ref, cubes_ref, out_ref):
    here = place_ref[0]
    order = (lambda n: reversed(range(n))) if reverse else range
    column = jnp.zeros((PIECE, DH), F32)
    for x in order(X):
        total = column
        for z in range(ZH):
            cube = piece(cubes_ref, (ZH_ORDER.index(z) * X + x) * PIECE)
            column = column + cube
            ahead = here < z if reverse else here > z
            total = total + jnp.where(ahead, cube, 0.0)
        for z in order(ZL):
            start = spot(x, z)
            out_ref[start : start + PIECE, :] = total.astype(BF16)
            total = total + piece(in_ref, start)


def inside_kernel(
    core_ref, q_ref, c_ref, sent_ref, k_ref, v_ref, gain_ref, q_near_ref, inside_ref, weighted_ref, near_gain_ref
):
    core = core_ref[0]
    mask = causal()
    assemble(core, q_ref, sent_ref, 0, q_near_ref)
    gain = gain_ref[:, part_of(core, PART)]
    near_gain_ref[...] = jnp.broadcast_to(gain, (8, PART))
    weighted_ref[part_of(core, ROWS), :] = c_ref[:, part_of(core, PART)].astype(F32) * gain
    weighted_ref[part_of(1 - core, ROWS), :] = arrived(core, sent_ref, 1).astype(F32) * gain
    for h in range(HALF):
        raw = dot(q_near_ref[:, at(h)], k_ref[:, at(h)], 1, 1)
        scores = jnp.where(mask, raw, 0.0).astype(BF16)
        inside_ref[:, at(h)] = dot(scores, v_ref[:, at(h)], 1, 0)


def rows_of(block):
    return [jnp.sum(block[i * ROWS : (i + 1) * ROWS].T, axis=0, keepdims=True) for i in range(CORES)]


def attended_kernel(q_ref, inside_ref, before_ref, weighted_ref, att_ref, sums_ref):
    squares = jnp.zeros((CHUNK, DH), F32)
    crossed = jnp.zeros((CHUNK, DH), F32)
    for h in range(HALF):
        att = inside_ref[:, at(h)] + dot(q_ref[:, at(h)], before_ref[at(h), :], 1, 0)
        att_ref[:, at(h)] = att
        squares = squares + att * att
        crossed = crossed + weighted_ref[:, at(h)] * att
    block = jnp.concatenate(rows_of(squares) + rows_of(crossed) + [jnp.zeros((4, ROWS), F32)], axis=0)
    for i in range(CORES * GROUPS):
        sums_ref[i * 8 : (i + 1) * 8, :] = block


def tall(rows):
    return jnp.concatenate([jnp.broadcast_to(row, (ROWS, ROWS)).T for row in rows], axis=0)


def token_scales(sums_ref):
    sums = sums_ref[0:8, :]
    for i in range(1, CORES * GROUPS):
        sums = sums + sums_ref[i * 8 : (i + 1) * 8, :]
    inverse_rows = lax.rsqrt(sums[0:2] / WIDTH_ALL + EPSILON)
    cubed_rows = inverse_rows * inverse_rows * inverse_rows * (sums[2:4] / WIDTH_ALL)
    return tall([inverse_rows[0:1], inverse_rows[1:2]]), tall([cubed_rows[0:1], cubed_rows[1:2]])


def grad_of(inverse, cubed, weighted_ref, att_ref, h):
    return (inverse * weighted_ref[:, at(h)] - cubed * att_ref[:, at(h)]).astype(BF16)


def products_kernel(sums_ref, att_ref, q_ref, weighted_ref, mine_ref):
    inverse, cubed = token_scales(sums_ref)
    for h in range(HALF):
        g = grad_of(inverse, cubed, weighted_ref, att_ref, h)
        mine_ref[at(h), :] = dot(q_ref[:, at(h)], g, 0, 0).astype(BF16)


def local_grads_kernel(
    core_ref, sums_ref, att_ref, weighted_ref, gain_ref, q_ref, k_ref, v_ref, before_ref,
    keep_ref, send_ref, gk_ref, gv_ref, normed_ref, gq_ref,
):
    mask = causal()
    inverse, cubed = token_scales(sums_ref)
    for h in range(HALF):
        q, k, v = q_ref[:, at(h)], k_ref[:, at(h)], v_ref[:, at(h)]
        normed_ref[:, at(h)] = (att_ref[:, at(h)] * inverse * gain_ref[0:1, at(h)]).astype(BF16)
        g = grad_of(inverse, cubed, weighted_ref, att_ref, h)
        scores = jnp.where(mask, dot(q, k, 1, 1), 0.0).astype(BF16)
        grad_scores = jnp.where(mask, dot(g, v, 1, 1), 0.0).astype(BF16)
        gq_ref[:, at(h)] = (dot(grad_scores, k, 1, 0) + dot(g, before_ref[at(h), :], 1, 1)).astype(BF16)
        gk_ref[:, at(h)] = dot(grad_scores, q, 0, 0)
        gv_ref[:, at(h)] = dot(scores, g, 0, 0)
    for out_ref, core in ((keep_ref, core_ref[0]), (send_ref, 1 - core_ref[0])):
        out_ref[0:ROWS, :] = normed_ref[part_of(core, ROWS), :]
        out_ref[ROWS : 2 * ROWS, :] = gq_ref[part_of(core, ROWS), :]


def last_kernel(core_ref, k_ref, v_ref, gk_part_ref, gv_part_ref, beyond_ref, keep_ref, send_ref):
    for h in range(HALF):
        beyond = beyond_ref[at(h), :]
        for out_ref, core in ((keep_ref, core_ref[0]), (send_ref, 1 - core_ref[0])):
            rows = part_of(core, ROWS)
            gk = gk_part_ref[rows, at(h)] + dot(v_ref[rows, at(h)], beyond, 1, 1)
            gv = gv_part_ref[rows, at(h)] + dot(k_ref[rows, at(h)], beyond, 1, 0)
            out_ref[0:ROWS, at(h)] = gk.astype(BF16)
            out_ref[ROWS : 2 * ROWS, at(h)] = gv.astype(BF16)


def join_kernel(core_ref, keep_ref, sent_ref, first_ref, second_ref):
    core = core_ref[0]
    for i, out_ref in enumerate((first_ref, second_ref)):
        out_ref[:, part_of(core, PART)] = keep_ref[i * ROWS : (i + 1) * ROWS, :]
        out_ref[:, part_of(1 - core, PART)] = arrived(core, sent_ref, i)


FLAT = (PART, DH)
TALL = (CHUNK, PART)
OUT = (ROWS, WIDTH)


def plane_swap(a):
    return lax.all_to_all(a, ("x", "zl"), 0, 0, axis_index_groups=PLANE, tiled=True)


def chips_scan(mine, reverse, beside_turn=lambda: None, beside_cubes=lambda: None):
    place = lax.axis_index("zh").reshape(1).astype(jnp.int32)
    turned = plane_swap(mine)
    (cube,) = call(cube_kernel, [(FLAT, BF16)], 0, BLOCK, [VMEM])(turned)
    cube, extra = lax.optimization_barrier((cube, beside_turn()))
    cubes = lax.all_to_all(cube, "zh", 0, 0, axis_index_groups=[list(ZH_ORDER)], tiled=True)
    scan = functools.partial(scan_kernel, reverse)
    (summed,) = call(scan, [(FLAT, BF16)], 0, 2 * BLOCK, [SMEM, VMEM, VMEM])(place, turned, cubes)
    summed, more = lax.optimization_barrier((summed, beside_cubes()))
    return plane_swap(summed), extra, more


def pair(a):
    return lax.all_gather(a, "core", axis=0, tiled=True)


def joined(core, keep, send):
    return call(join_kernel, [(OUT, BF16), (OUT, BF16)], 0, 4 * BLOCK, [SMEM, VMEM, VMEM])(core, keep, pair(send))


def swapped(core, a, b):
    (send,) = call(
        pack_kernel, [(TALL, BF16)], 0, 2 * BLOCK, [SMEM, ANY, ANY], [pltpu.SemaphoreType.DMA((2,))], ANY
    )(core, a, b)
    return pair(send)


def local(q, k, v, gain, c):
    core = lax.axis_index("core").reshape(1).astype(jnp.int32)
    gain = gain.reshape(1, WIDTH)
    k, v, mine = call(
        states_kernel, [(TALL, BF16), (TALL, BF16), (FLAT, BF16)], MATMUL, 5 * BLOCK, [SMEM] + [VMEM] * 3
    )(core, k, v, swapped(core, k, v))
    sent = swapped(core, q, c)

    def prepare():
        return call(
            inside_kernel,
            [(TALL, BF16), (TALL, F32), (TALL, F32), ((8, PART), F32)],
            4 * MATMUL, 12 * BLOCK, [SMEM] + [VMEM] * 6,
        )(core, q, c, sent, k, v, gain)

    before, _, (q_near, inside, weighted, near_gain) = chips_scan(mine, False, lambda: None, prepare)
    att, sums = call(
        attended_kernel, [(TALL, F32), ((CORES * GROUPS * 8, ROWS), F32)], MATMUL, 10 * BLOCK, [VMEM] * 4
    )(q_near, inside, before, weighted)
    sums = lax.all_to_all(sums, ("core", "head"), 0, 0, axis_index_groups=[SUM_ORDER], tiled=True)
    (mine,) = call(products_kernel, [(FLAT, BF16)], MATMUL, 6 * BLOCK, [VMEM] * 4)(sums, att, q_near, weighted)
    keep, send, gk_part, gv_part = call(
        local_grads_kernel,
        [(TALL, BF16), (TALL, BF16), (TALL, F32), (TALL, F32)],
        12 * MATMUL, 18 * BLOCK, [SMEM] + [VMEM] * 8, [pltpu.VMEM(TALL, BF16)] * 2,
    )(core, sums, att, weighted, near_gain, q_near, k, v, before)
    beyond, _, (gk_part, gv_part, normed, gq) = chips_scan(
        mine, True, lambda: None, lambda: (gk_part, gv_part) + tuple(joined(core, keep, send))
    )
    keep, send = call(last_kernel, [(TALL, BF16), (TALL, BF16)], 2 * MATMUL, 11 * BLOCK, [SMEM] + [VMEM] * 5)(
        core, k, v, gk_part, gv_part, beyond
    )
    gk, gv = joined(core, keep, send)
    return normed, gq, gk, gv


def solution(mesh):
    fine = Mesh(mesh.devices.reshape(X, ZH, ZL, CORES, GROUPS), ("x", "zh", "zl", "core", "head"))
    block = P(("x", "zh", "zl", "core"), "head")
    return jax.shard_map(
        local, mesh=fine, in_specs=(block, block, block, P("head"), block), out_specs=(block,) * 4, check_vma=False
    )
```
